32 devices in a mesh: gx: 8 (over y, x, core), gy: 4 (over z).
Axes of the slice: x: 2, y: 2, z: 4, core: 2. Of those that a mesh axis runs over, the one named last changes fastest.
Arguments:
- thermal_anomaly_grid: float32 [30, 128, 1024], P(None, 'gy', 'gx'), may hold values from -5 to 5
- relative_moisture: float32 [30, 128, 1024], P(None, 'gy', 'gx'), may hold values from 0.05 to 1
- overcast_share: float32 [30, 128, 1024], P(None, 'gy', 'gx'), may hold values from 0 to 1
- sun_angle_projection: float32 [128, 1024], P('gy', 'gx'), may hold values from 0.1 to 1
- daylight_mask: int32 [8, 128], P('gx', 'gy'), may hold values 0 or 1
- radiator_owner_position: int32 [8, 128, 1], P('gx', 'gy'), may hold values from 0 to 7; in each aligned block of 32 rows (0 to 31, 32 to 63, ..., all dimensions but the last counted through in order) at most 8 rows name the same one
- molecular_opacity_lookup: bfloat16 [30, 140, 128], replicated, may hold values from 0.019897461 to 1.5
- condensed_opacity_per_share: float32 [140], replicated, may hold values from 0.05 to 1
- planck_emission_factor: float32 [140], replicated, may hold values from 0.2 to 1
- insolation_quadrature_factor: float32 [140], replicated, may hold values from 0.2 to 2
Outputs:
- advanced_anomaly_grid: float32 [30, 128, 1024], P(None, 'gy', 'gx')
- humidity_next: float32 [30, 128, 1024], P(None, 'gy', 'gx')
- ground_irradiance_slots: float32 [4, 8, 8, 8, 128], P('gy', 'gx')
The draws below stay inside these ranges and needn't reach their ends.
Inputs may be any that keep to these rules, and one draw needn't show every extreme that they name: `radiator_owner_position`: among the 32 blocks of one device, at most 8 name the same host, and some device's blocks name one host exactly 8 times.
All inputs are finite; a program needn't handle non-finite values. No bound on the sum of `daylight_mask` on one device may be relied on, other than what follows from the above.
Results may differ from the reference program's by a relative error of at most 0.0034.
Values may be sent and summed in bfloat16 or wider, within the bound.
No kernel may reach another device: no remote copies, remote signals or barrier semaphores. Data moves between devices by JAX's collectives and lax.ppermute only.
A program may use at most 128 MiB of HBM per device.

```python
import math
import jax
import jax.numpy as jnp
import numpy as np
from jax import lax

STRATA_NUMBER = 30
G = 140
NT = 16
NQ = 8
CXT = 128
CYT = 32
NODES = 128
CAP = 8
EASTWARD_SPAN = 1024
NORTHWARD_SPAN = 128
N_GX = 8
N_GY = 4


def place_ends(result, own_key, low, high):
    dims = result.shape
    spot = [jax.random.randint(jax.random.fold_in(own_key, axis), (), 0, dims[axis]) for axis in range(len(dims))]
    result = result.at[tuple(spot)].set(low)
    longest = dims.index(max(dims))
    spot[longest] = (spot[longest] + 1) % dims[longest]
    return result.at[tuple(spot)].set(high)


def level_of(key, dims, pieces, low, largest):
    factor_of, own = 1.0, jax.random.fold_in(key, 6)
    for axis_at, parts in pieces:
        steps = jnp.exp(jax.random.uniform(jax.random.fold_in(own, axis_at), (parts,), jnp.float32, low / len(pieces), largest / len(pieces)))
        factor_of = factor_of * jnp.repeat(steps, dims[axis_at] // parts).reshape([-1 if axis == axis_at else 1 for axis in range(len(dims))])
    return factor_of


def shared_out(stream_key, own, number, rows, amount, top, most, skew):
    order = jax.random.permutation(stream_key, amount)
    packed, usual = load_shares(amount, rows * top, most, skew, True), load_shares(amount, rows * top, most, skew, False)
    places = jnp.arange(amount)

    def named(tallies, rotation):
        used = int((tallies > 0).sum())
        fixed = max(1, used // 4)
        moved = fixed + (places - fixed + rotation * (used - fixed)) % max(1, amount - fixed)
        return jnp.zeros((amount,), jnp.int32).at[order[jnp.where(places < fixed, places, moved)]].set(jnp.asarray(tallies, jnp.int32))

    tallies = jnp.where(number % 4 == 0, named(packed, number // 4), named(usual, number - number // 4 - 1))
    mixed = jax.random.permutation(jax.random.fold_in(own, 3), amount)
    donor, receiver = mixed[0:amount // 2 * 2:2], mixed[1:amount // 2 * 2:2]
    margin = jnp.minimum(tallies[donor] - 1, most - tallies[receiver]) // 2
    margin = jnp.where((donor == order[0]) | (receiver == order[0]) | (tallies[receiver] == 0), 0, jnp.maximum(margin, 0))
    moved = jax.random.randint(jax.random.fold_in(own, 4), (amount // 2,), 0, 1 << 20) % (margin + 1)
    tallies = tallies.at[donor].add(-moved).at[receiver].add(moved)
    members = jnp.searchsorted(jnp.cumsum(tallies), jnp.arange(rows * top), side="right").astype(jnp.int32)
    listing = members.reshape(top, rows).T
    listing = listing[jax.random.permutation(jax.random.fold_in(own, 1), rows)]
    rotation = jax.random.randint(jax.random.fold_in(own, 2), (rows, 1), 0, top)
    return jnp.take_along_axis(listing, (jnp.arange(top)[None, :] + rotation) % top, axis=1)


def load_shares(number_of, total, bound, lean, full):
    weights = [(1 << 20) // math.isqrt(grade ** lean) + 1 for grade in range(1, number_of + 1)]
    largest = bound if full else min(bound, max(-(-total // number_of), total * weights[0] // sum(weights)))
    least = 1 if total - largest >= number_of - 1 else 0
    holding, rest = [largest] + [least] * (number_of - 1), total - largest - least * (number_of - 1)
    while rest > 0:
        free = [i for i in range(1, number_of) if holding[i] < largest] or [i for i in range(1, number_of) if holding[i] < bound]
        whole, remaining = sum([weights[i] for i in free]), rest
        for i in free:
            more = min(bound - holding[i], max(1, remaining * weights[i] // whole), rest)
            holding[i] = holding[i] + more
            rest = rest - more
    return np.array(holding)


def bell_draw(stream_key, extent, deviation, most, pieces=(), held_as=jnp.bfloat16):
    values = jax.random.normal(stream_key, extent, jnp.float32) * deviation
    if len(pieces) > 0:
        values = level_of(stream_key, extent, pieces, -0.22, 0.18) * values
    return jnp.clip(values, min=-most, max=most).astype(held_as)


def setup_inputs(seed: int = 0) -> dict:
    arg_keys = jax.random.split(jax.random.key(seed), 11)
    thermal_anomaly_grid = bell_draw(arg_keys[0], (STRATA_NUMBER, NORTHWARD_SPAN, EASTWARD_SPAN), 1.0, 5.0, ((1, 4), (2, 8)), jnp.float32)
    relative_moisture = jnp.clip(0.05 + 0.95 * jax.random.uniform(arg_keys[1], (STRATA_NUMBER, NORTHWARD_SPAN, EASTWARD_SPAN), jnp.float32) ** level_of(arg_keys[1], (STRATA_NUMBER, NORTHWARD_SPAN, EASTWARD_SPAN), ((1, 4), (2, 8)), -0.2, 0.2), 0.05, 1.0)
    overcast_share = jnp.clip(1.0 * jax.random.uniform(arg_keys[2], (STRATA_NUMBER, NORTHWARD_SPAN, EASTWARD_SPAN), jnp.float32) ** level_of(arg_keys[2], (STRATA_NUMBER, NORTHWARD_SPAN, EASTWARD_SPAN), ((1, 4), (2, 8)), -0.2, 0.2), 0.0, 1.0)
    sun_angle_projection = jnp.clip(0.1 + 0.9 * jax.random.uniform(arg_keys[3], (NORTHWARD_SPAN, EASTWARD_SPAN), jnp.float32) ** level_of(arg_keys[3], (NORTHWARD_SPAN, EASTWARD_SPAN), ((0, 4), (1, 8)), -0.2, 0.2), 0.1, 1.0)
    daylight_mask = place_ends((jax.random.randint(arg_keys[4], (N_GX, NORTHWARD_SPAN), 0, 2) < 1).astype(jnp.int32), jax.random.fold_in(arg_keys[4], 1), 0, 1)
    radiator_owner_position_keys = jax.random.split(jax.random.fold_in(arg_keys[5], 1), N_GX * NORTHWARD_SPAN // CYT)
    radiator_owner_position_turns = jax.random.permutation(jax.random.fold_in(arg_keys[5], 3), N_GX * NORTHWARD_SPAN // CYT)
    radiator_owner_position = jax.vmap(lambda own, number: shared_out(jax.random.fold_in(arg_keys[5], 2), own, number, CYT, N_GX, 1, CAP, 2))(radiator_owner_position_keys, radiator_owner_position_turns).reshape((N_GX, NORTHWARD_SPAN, 1))
    molecular_opacity_lookup = jnp.clip(jnp.exp(jax.random.uniform(arg_keys[6], (STRATA_NUMBER, G, NODES), jnp.float32, math.log(0.019897461), math.log(1.5))), 0.019897461, 1.5).astype(jnp.bfloat16)
    condensed_opacity_per_share = jnp.clip(jnp.exp(jax.random.uniform(arg_keys[7], (G,), jnp.float32, math.log(0.05), math.log(1.0))), 0.05, 1.0)
    planck_emission_factor = jnp.clip(jnp.exp(jax.random.uniform(arg_keys[8], (G,), jnp.float32, math.log(0.2), math.log(1.0))), 0.2, 1.0)
    insolation_quadrature_factor = jnp.clip(jnp.exp(jax.random.uniform(arg_keys[9], (G,), jnp.float32, math.log(0.2), math.log(2.0))), 0.2, 2.0)
    return {"thermal_anomaly_grid": thermal_anomaly_grid, "relative_moisture": relative_moisture, "overcast_share": overcast_share, "sun_angle_projection": sun_angle_projection, "daylight_mask": daylight_mask, "radiator_owner_position": radiator_owner_position, "molecular_opacity_lookup": molecular_opacity_lookup, "condensed_opacity_per_share": condensed_opacity_per_share, "planck_emission_factor": planck_emission_factor, "insolation_quadrature_factor": insolation_quadrature_factor}


diffusion = 0.2
diffusivity = 1.66


def stencil(bordered_grid):
    centre = bordered_grid[:, :, 1:-1, 1:-1]
    beside_all = bordered_grid[:, :, 2:, 1:-1] + bordered_grid[:, :, :-2, 1:-1] + bordered_grid[:, :, 1:-1, 2:] + bordered_grid[:, :, 1:-1, :-2]
    return centre + diffusion * (beside_all - 4.0 * centre)


def optical_depth(layer, table_layer, condensed_opacity_per_share):
    air_temp, moisture, condensate = layer[0], layer[1], layer[2]
    temp_nodes = jnp.arange(NT, dtype=jnp.float32)
    humid_nodes = jnp.arange(NQ, dtype=jnp.float32)
    temp_pos = jnp.clip((air_temp + 3.0) * ((NT - 1.0) / 6.0), 0.0, NT - 1.0)
    humid_pos = jnp.clip(moisture * (NQ - 1.0), 0.0, NQ - 1.0)
    temp_hat = jnp.maximum(0.0, 1.0 - jnp.abs(temp_pos[None, :] - temp_nodes[:, None]))
    humid_hat = jnp.maximum(0.0, 1.0 - jnp.abs(humid_pos[None, :] - humid_nodes[:, None]))
    weights = (temp_hat[:, None, :] * humid_hat[None, :, :]).reshape(NT * NQ, -1).astype(jnp.bfloat16)
    gas_depth = jnp.dot(table_layer, weights, preferred_element_type=jnp.float32)
    return gas_depth + condensed_opacity_per_share[:, None] * condensate[None, :]


def column_physics(prognostic_bundle, zenith, incident, molecular_opacity_lookup, condensed_opacity_per_share, planck_emission_factor, insolation_quadrature_factor):
    layers = jnp.transpose(prognostic_bundle, (1, 0, 2))
    gpoints = planck_emission_factor.shape[0]

    def downward(carry, inputs):
        long_down, short_down = carry
        layer, table_layer = inputs
        depth = optical_depth(layer, table_layer, condensed_opacity_per_share)
        through = jnp.exp(-diffusivity * depth)
        source = planck_emission_factor[:, None] * (1.0 + 0.25 * layer[0][None, :])
        long_next = long_down * through + (1.0 - through) * source
        short_next = short_down * jnp.exp(-depth / zenith[None, :])
        gained = jnp.sum(long_down - long_next + short_down - short_next, axis=0)
        return (long_next, short_next), gained

    def upward(long_up, inputs):
        layer, table_layer = inputs
        depth = optical_depth(layer, table_layer, condensed_opacity_per_share)
        through = jnp.exp(-diffusivity * depth)
        source = planck_emission_factor[:, None] * (1.0 + 0.25 * layer[0][None, :])
        long_next = long_up * through + (1.0 - through) * source
        return long_next, jnp.sum(long_up - long_next, axis=0)

    start_long = jnp.zeros((gpoints, prognostic_bundle.shape[2]), jnp.float32)
    start_short = insolation_quadrature_factor[:, None] * incident[None, :]
    bottom, down_gain = lax.scan(downward, (start_long, start_short), (layers, molecular_opacity_lookup))
    start_up = planck_emission_factor[:, None] * (1.0 + 0.25 * layers[-1, 0][None, :])
    top_up, up_gain = lax.scan(upward, start_up, (layers, molecular_opacity_lookup), reverse=True)
    heating = (2.0 / gpoints) * (down_gain + up_gain)
    ground_irradiance_result = jnp.sum(bottom[0] + bottom[1], axis=0) / gpoints
    return heating, ground_irradiance_result


def reference(thermal_anomaly_grid, relative_moisture, overcast_share, sun_angle_projection, daylight_mask, radiator_owner_position, molecular_opacity_lookup, condensed_opacity_per_share, planck_emission_factor, insolation_quadrature_factor):
    gridded_quantities = jnp.stack((thermal_anomaly_grid, relative_moisture))
    laplacian_blurred_grid = stencil(jnp.pad(gridded_quantities, ((0, 0), (0, 0), (1, 1), (1, 1))))
    prognostic_bundle = jnp.stack((thermal_anomaly_grid, relative_moisture, overcast_share)).astype(jnp.bfloat16)
    prognostic_bundle = lax.optimization_barrier(prognostic_bundle).astype(jnp.float32)
    lit_columns = jnp.repeat(jnp.transpose(daylight_mask), CXT, axis=1).astype(jnp.float32)
    light = jnp.stack((sun_angle_projection, sun_angle_projection * lit_columns)).astype(jnp.bfloat16)
    light = lax.optimization_barrier(light).astype(jnp.float32)

    def one_row(row_index):
        start = row_index * CYT
        rows = lax.dynamic_slice_in_dim(prognostic_bundle, start, CYT, 2).reshape(3, STRATA_NUMBER, CYT * EASTWARD_SPAN)
        shine = lax.dynamic_slice_in_dim(light, start, CYT, 1).reshape(2, CYT * EASTWARD_SPAN)
        heating, ground_irradiance_result = column_physics(rows, shine[0], shine[1], molecular_opacity_lookup, condensed_opacity_per_share, planck_emission_factor, insolation_quadrature_factor)
        return heating.reshape(STRATA_NUMBER, CYT, EASTWARD_SPAN), ground_irradiance_result.reshape(CYT, EASTWARD_SPAN)

    heat_rows, surface_rows = lax.map(one_row, jnp.arange(N_GY, dtype=jnp.int32))
    warming_overall = jnp.transpose(heat_rows, (1, 0, 2, 3)).reshape(STRATA_NUMBER, NORTHWARD_SPAN, EASTWARD_SPAN)
    advanced_anomaly_grid = laplacian_blurred_grid[0] + warming_overall
    hosts = radiator_owner_position[:, :, 0].reshape(N_GX, N_GY, CYT)
    earlier = jnp.arange(CYT)[None, :] < jnp.arange(CYT)[:, None]
    same = hosts[:, :, :, None] == hosts[:, :, None, :]
    rank = jnp.sum(jnp.logical_and(same, earlier[None, None]), axis=3).astype(jnp.int32)
    host_ids = jnp.arange(N_GX, dtype=jnp.int32)[None, None, :, None, None]
    slot_ids = jnp.arange(CAP, dtype=jnp.int32)[None, None, None, :, None]
    pick = jnp.logical_and(hosts[:, :, None, None, :] == host_ids, rank[:, :, None, None, :] == slot_ids).astype(jnp.float32)
    profile_groups = surface_rows.reshape(N_GY, CYT, N_GX, CXT)
    ground_irradiance_slots = jnp.einsum("srhkb,rbsx->rhskx", pick, profile_groups, precision=lax.Precision.HIGHEST)
    return advanced_anomaly_grid, laplacian_blurred_grid[1], ground_irradiance_slots
```

```python
import functools
import math

import jax
import jax.numpy as jnp
from jax import lax
from jax.experimental import pallas as pl
from jax.experimental.pallas import tpu as pltpu
from jax.sharding import PartitionSpec as P

NT = 16
NQ = 8
NODES = NT * NQ
LANES = 128
ROWS = 8

diffusion = 0.2
diffusivity = 1.66
LOG2E = math.log2(math.e)

BF = jnp.bfloat16
F32 = jnp.float32


def rounded(x):
    return x.astype(BF).astype(F32)


def unrolled(count, most, body, carry):
    steps = max(n for n in range(1, most + 1) if count % n == 0)

    def several(o, carry):
        for k in range(steps):
            carry = body(o * steps + k, carry)
        return carry

    return lax.fori_loop(0, count // steps, several, carry)


def column_kernel(
    gpoints,
    t_ref,
    q_ref,
    c_ref,
    mu_ref,
    lit_ref,
    table_ref,
    cond_ref,
    planck_ref,
    insol_ref,
    total_ref,
    heat_ref,
    surface_ref,
    table_s,
    th_s,
    qh_s,
    dt_s,
    c_s,
    tr_s,
    beam_s,
    down_s,
    up_s,
):
    levels = t_ref.shape[0]
    padded = table_s.shape[1]
    tiles = padded // 16

    @pl.when(pl.program_id(0) == 0)
    def _():
        def prepare(l, _):
            layer = table_ref[l].astype(F32) * (-diffusivity * LOG2E)
            table_s[l] = jnp.concatenate(
                [layer, jnp.zeros((padded - gpoints, NODES), F32)], axis=0
            ).astype(BF)
            return 0

        lax.fori_loop(0, levels, prepare, 0)

    def hats(l, _):
        t = rounded(t_ref[l])
        q = rounded(q_ref[l])
        t_pos = jnp.clip((t + 3.0) * ((NT - 1.0) / 6.0), 0.0, NT - 1.0)
        q_pos = jnp.clip(q * (NQ - 1.0), 0.0, NQ - 1.0)
        for i in range(NT):
            th_s[l, i] = jnp.maximum(0.0, 1.0 - jnp.abs(t_pos - float(i)))
        for j in range(NQ):
            qh_s[l, j] = jnp.maximum(0.0, 1.0 - jnp.abs(q_pos - float(j)))
        following = rounded(t_ref[jnp.minimum(l + 1, levels - 1)])
        dt_s[l] = 0.25 * (t - following)
        c_s[l] = rounded(c_ref[l])
        return 0

    lax.fori_loop(0, levels, hats, 0)

    def spread(ref, index, row):
        return jnp.broadcast_to(ref[*index, pl.ds(row, 1), :], (ROWS, LANES))

    def wide(ref, index, row):
        one = spread(ref, index, row)
        return jnp.concatenate([one, one], axis=0).astype(BF)

    def weights(l, row):
        qh = jnp.concatenate(
            [qh_s[l, j, pl.ds(row, 1), :] for j in range(NQ)] * 2, axis=0
        ).astype(BF)
        parts = []
        for m in range(NT // 2):
            pair = jnp.concatenate(
                [spread(th_s, (l, 2 * m), row), spread(th_s, (l, 2 * m + 1), row)], axis=0
            ).astype(BF)
            parts.append(pair * qh)
        cloud = wide(c_s, (l,), row)
        return jnp.concatenate(parts + [cloud] * (NODES // 16), axis=0)

    def both(make):
        return jnp.concatenate([make(0), make(1)], axis=1)

    def per_point(ref, k):
        tile = ref[16 * k : 16 * k + 16, :]
        return jnp.concatenate([tile, tile], axis=1)

    def put(ref, l, first, parts):
        pairs = [parts[k] + parts[k + 1] for k in range(0, tiles - 1, 2)]
        if tiles % 2:
            pairs.append(parts[-1])
        total = sum(pair.astype(F32) for pair in pairs)
        total = total[:ROWS] + total[ROWS:]
        for h in range(2):
            at = pl.ds(pl.multiple_of((first + h) * ROWS, ROWS), ROWS)
            ref[l, at, :] = total[:, h * LANES : (h + 1) * LANES]

    def pair_of_rows(p, _):
        first = 2 * p

        def inverse_of(h):
            one = (1.0 / diffusivity) / rounded(mu_ref[pl.ds(first + h, 1), :])
            return jnp.broadcast_to(one, (16, LANES)).astype(BF)

        inverse = both(inverse_of)
        lit = both(lambda h: wide(lit_ref, (), first + h))
        start = both(lambda h: wide(t_ref, (0,), first + h)) * jnp.asarray(-0.25, BF) - jnp.asarray(
            1.0, BF
        )

        def transmit(l, _):
            rhs = both(lambda h: weights(l, first + h))
            lhs = jnp.concatenate([table_s[l], cond_ref[...]], axis=1)
            depth = jnp.dot(lhs, rhs, preferred_element_type=F32)
            for k in range(tiles):
                at = slice(16 * k, 16 * k + 16)
                part = depth[at].astype(BF)
                tr_s[l, at] = jnp.exp2(part)
                beam_s[l, at] = jnp.exp2(part * inverse)
            return 0

        def downward(l, carry):
            long, short = list(carry[0]), list(carry[1])
            step = both(lambda h: wide(dt_s, (l,), first + h))
            parts = []
            for k in range(tiles):
                at = slice(16 * k, 16 * k + 16)
                kept = tr_s[l, at] * long[k]
                short[k] = short[k] * beam_s[l, at]
                parts.append(kept + short[k])
                long[k] = kept + per_point(planck_ref, k) * step
            put(down_s, l, first, parts)
            return tuple(long), tuple(short)

        def upward(n, long):
            l = levels - 1 - n
            step = both(lambda h: wide(dt_s, (jnp.maximum(l - 1, 0),), first + h))
            long = list(long)
            parts = []
            for k in range(tiles):
                kept = tr_s[l, slice(16 * k, 16 * k + 16)] * long[k]
                parts.append(kept)
                long[k] = kept + per_point(planck_ref, k) * step
            put(up_s, l, first, parts)
            return tuple(long)

        unrolled(levels, 6, transmit, 0)
        unrolled(
            levels,
            6,
            downward,
            (
                tuple(per_point(planck_ref, k) * start for k in range(tiles)),
                tuple(per_point(insol_ref, k) * lit for k in range(tiles)),
            ),
        )
        zero = jnp.zeros((16, 2 * LANES), BF)
        unrolled(levels, 6, upward, (zero,) * tiles)
        return 0

    lax.fori_loop(0, ROWS // 2, pair_of_rows, 0)

    planck_total = total_ref[0, 0]
    insol_total = total_ref[0, 1]

    def gathered(ref, l):
        return sum(ref[l, pl.ds(k, ROWS, stride=ROWS), :] for k in range(ROWS))

    def finish(l, down_in):
        source = (1.0 + 0.25 * rounded(t_ref[l])) * planck_total
        after = jnp.minimum(l + 1, levels - 1)
        source_after = (1.0 + 0.25 * rounded(t_ref[after])) * planck_total
        down_out = gathered(down_s, l) + source
        up_out = source - gathered(up_s, l)
        up_in = jnp.where(l == levels - 1, source, source_after - gathered(up_s, after))
        heat_ref[l] = (2.0 / gpoints) * (down_in - down_out + up_in - up_out)
        return down_out

    bottom = lax.fori_loop(0, levels, finish, rounded(lit_ref[...]) * insol_total)
    surface_ref[...] = bottom * (1.0 / gpoints)


def halves(x):
    high = x.astype(BF)
    return high, (x - high.astype(F32)).astype(BF)


def whole(x):
    return pl.BlockSpec(x.shape, lambda i: (0,) * x.ndim)


def radiate(t, q, c, mu, lit, table, cond, planck, insol):
    levels, rows, width = t.shape
    gpoints = table.shape[1]
    padded = -(-gpoints // 16) * 16

    def spread(x):
        return jnp.broadcast_to(jnp.pad(x.astype(BF), (0, padded - gpoints))[:, None], (padded, LANES))

    cond_high, cond_low = halves(cond * (-diffusivity * LOG2E))
    cond_tile = jnp.pad(
        jnp.stack([cond_high, cond_low], axis=1), ((0, padded - gpoints), (0, NODES - 2))
    )
    total = jnp.stack([jnp.sum(rounded(planck)), jnp.sum(rounded(insol))])[None]
    grid3 = pl.BlockSpec((levels, ROWS, width), lambda i: (0, i, 0))
    grid2 = pl.BlockSpec((ROWS, width), lambda i: (i, 0))

    tall_planck, tall_insol = spread(planck), spread(insol)
    return pl.pallas_call(
        functools.partial(column_kernel, gpoints),
        grid=(rows // ROWS,),
        in_specs=[
            grid3,
            grid3,
            grid3,
            grid2,
            grid2,
            whole(table),
            whole(cond_tile),
            whole(tall_planck),
            whole(tall_insol),
            pl.BlockSpec(memory_space=pltpu.SMEM),
        ],
        out_specs=[grid3, grid2],
        out_shape=[
            jax.ShapeDtypeStruct((levels, rows, width), F32),
            jax.ShapeDtypeStruct((rows, width), F32),
        ],
        scratch_shapes=[
            pltpu.VMEM((levels, padded, NODES), BF),
            pltpu.VMEM((levels, NT, ROWS, LANES), F32),
            pltpu.VMEM((levels, NQ, ROWS, LANES), F32),
            pltpu.VMEM((levels, ROWS, LANES), F32),
            pltpu.VMEM((levels, ROWS, LANES), F32),
            pltpu.VMEM((levels, padded, 2 * LANES), BF),
            pltpu.VMEM((levels, padded, 2 * LANES), BF),
            pltpu.VMEM((levels, ROWS * ROWS, LANES), F32),
            pltpu.VMEM((levels, ROWS * ROWS, LANES), F32),
        ],
        compiler_params=pltpu.CompilerParams(vmem_limit_bytes=40 * 1024 * 1024),
        cost_estimate=pl.CostEstimate(
            flops=2 * levels * padded * 256 * rows * width,
            bytes_accessed=4 * 4 * levels * rows * width,
            transcendentals=2 * levels * padded * rows * width,
        ),
        name="columns",
    )(t, q, c, mu, lit, table, cond_tile, tall_planck, tall_insol, total)


def edge_kernel(t_ref, q_ref, sides_ref, low_ref, high_ref):
    levels, rows, width = t_ref.shape
    lane = lax.broadcasted_iota(jnp.int32, (rows, width), 1)

    def body(l, packed):
        for k, ref in enumerate((t_ref, q_ref)):
            n = k * levels + l
            v = ref[l]
            low_ref[pl.ds(n, 1), :] = v[:1]
            high_ref[pl.ds(n, 1), :] = v[rows - 1 :]
            packed = jnp.where(lane // 2 == n, pltpu.roll(v, 2 * n + 1, axis=1), packed)
        return packed

    sides_ref[...] = unrolled(levels, 6, body, jnp.zeros((rows, width), F32))


def edges(t, q):
    levels, rows, width = t.shape
    line = jax.ShapeDtypeStruct((2 * levels, width), F32)
    return pl.pallas_call(
        edge_kernel,
        out_shape=[jax.ShapeDtypeStruct((rows, width), F32), line, line],
        name="edges",
    )(t, q)


def stencil_kernel(
    levels, t_ref, q_ref, heat_ref, west_ref, east_ref, south_ref, north_ref, t_out, q_out
):
    count, rows, width = t_ref.shape
    lane = lax.broadcasted_iota(jnp.int32, (rows, width), 1)
    row = lax.broadcasted_iota(jnp.int32, (rows, width), 0)
    sides = jnp.where(
        lane % 2 == 0,
        pltpu.roll(east_ref[...], width - 1, axis=1),
        pltpu.roll(west_ref[...], 1, axis=1),
    )

    def smoothed(v, n):
        halo = pltpu.roll(sides, width - 1 - 2 * n, axis=1)
        west = jnp.where(lane == 0, halo, pltpu.roll(v, 1, axis=1))
        east = jnp.where(lane == width - 1, halo, pltpu.roll(v, width - 1, axis=1))
        south = jnp.where(row == 0, south_ref[pl.ds(n, 1), :], pltpu.roll(v, 1, axis=0))
        north = jnp.where(row == rows - 1, north_ref[pl.ds(n, 1), :], pltpu.roll(v, rows - 1, axis=0))
        return v + diffusion * (((north + south) + (east + west)) - 4.0 * v)

    for j in range(count):
        l = pl.program_id(0) * count + j
        t_out[j] = smoothed(t_ref[j], l) + heat_ref[j]
        q_out[j] = smoothed(q_ref[j], levels + l)


def diffuse(t, q, heating, west, east, south, north):
    levels, rows, width = t.shape
    count = max(n for n in range(1, 7) if levels % n == 0)
    block = pl.BlockSpec((count, rows, width), lambda i: (i, 0, 0))
    out = jax.ShapeDtypeStruct(t.shape, F32)
    return pl.pallas_call(
        functools.partial(stencil_kernel, levels),
        grid=(levels // count,),
        in_specs=[block, block, block, whole(west), whole(east), whole(south), whole(north)],
        out_specs=[block, block],
        out_shape=[out, out],
        name="diffuse",
    )(t, q, heating, west, east, south, north)


def neighbours(low_edge, high_edge, axis):
    count = lax.axis_size(axis)
    forward = [(i, i + 1) for i in range(count - 1)]
    backward = [(target, source) for source, target in forward]
    return lax.ppermute(high_edge, axis, forward), lax.ppermute(low_edge, axis, backward)


def block_rank(hosts):
    count = hosts.shape[-1]
    earlier = jnp.arange(count)[None, :] < jnp.arange(count)[:, None]
    same = hosts[:, None] == hosts[None, :]
    return jnp.sum(jnp.logical_and(same, earlier), axis=-1)


def on_device(
    thermal_anomaly_grid,
    relative_moisture,
    overcast_share,
    sun_angle_projection,
    daylight_mask,
    radiator_owner_position,
    molecular_opacity_lookup,
    condensed_opacity_per_share,
    planck_emission_factor,
    insolation_quadrature_factor,
):
    host_count = lax.axis_size("gx")
    t, q = thermal_anomaly_grid, relative_moisture
    blocks = t.shape[1]
    capacity = max(2, (2 * blocks + host_count - 1) // host_count)

    sides, low, high = edges(t, q)
    west, east = neighbours(sides, sides, "gx")
    south, north = neighbours(low, high, "gy")

    lit = sun_angle_projection * daylight_mask[0].astype(F32)[:, None]
    heating, surface = radiate(
        t,
        q,
        overcast_share,
        sun_angle_projection,
        lit,
        molecular_opacity_lookup,
        condensed_opacity_per_share,
        planck_emission_factor,
        insolation_quadrature_factor,
    )

    hosts = radiator_owner_position[0, :, 0]
    slot = hosts * capacity + block_rank(hosts)
    chosen = (jnp.arange(host_count * capacity)[:, None] == slot[None, :]).astype(F32)
    sent = jnp.dot(chosen, surface, precision=lax.Precision.HIGHEST)
    slots = lax.all_to_all(
        sent.reshape(host_count, capacity, surface.shape[1]),
        "gx",
        split_axis=0,
        concat_axis=0,
        tiled=True,
    )

    t_next, q_next = diffuse(t, q, heating, west, east, south, north)
    return t_next, q_next, slots[None, None]


def solution(mesh):
    placed = (
        P(None, "gy", "gx"),
        P(None, "gy", "gx"),
        P(None, "gy", "gx"),
        P("gy", "gx"),
        P("gx", "gy"),
        P("gx", "gy", None),
        P(),
        P(),
        P(),
        P(),
    )
    return jax.shard_map(
        on_device,
        mesh=mesh,
        in_specs=placed,
        out_specs=(P(None, "gy", "gx"), P(None, "gy", "gx"), P("gy", "gx", None, None, None)),
        check_vma=False,
    )
```

```python
import functools
import math

import jax
import jax.numpy as jnp
from jax import lax
from jax.experimental import pallas as pl
from jax.experimental.pallas import tpu as pltpu
from jax.sharding import PartitionSpec as P

NT = 16
NQ = 8
NODES = NT * NQ
LANES = 128
ROWS = 8

diffusion = 0.2
diffusivity = 1.66
LOG2E = math.log2(math.e)

BF = jnp.bfloat16
F32 = jnp.float32


def rounded(x):
    return x.astype(BF).astype(F32)


def unrolled(count, most, body, carry):
    steps = max(n for n in range(1, most + 1) if count % n == 0)

    def several(o, carry):
        for k in range(steps):
            carry = body(o * steps + k, carry)
        return carry

    return lax.fori_loop(0, count // steps, several, carry)


def column_kernel(
    gpoints,
    capacity,
    hosts_ref,
    daylight_ref,
    t_ref,
    q_ref,
    c_ref,
    mu_ref,
    table_ref,
    planck_ref,
    insol_ref,
    cond_ref,
    heat_ref,
    slots_ref,
    table_s,
    cond_s,
    planck_s,
    insol_s,
    inverse_s,
    lit_s,
    points_s,
    th_s,
    qh_s,
    dt_s,
    tr_s,
    beam_s,
    down_s,
    up_s,
    surface_s,
    taken_s,
):
    levels, rows, _ = t_ref.shape
    padded = table_s.shape[1]
    tiles = padded // 16
    groups = rows // ROWS
    pairs = rows // 2

    def prepare(l, _):
        layer = table_ref[l].astype(F32) * (-diffusivity * LOG2E)
        table_s[l] = jnp.concatenate(
            [layer, jnp.zeros((padded - gpoints, NODES), F32)], axis=0
        ).astype(BF)
        return 0

    unrolled(levels, 3, prepare, 0)

    points_s[...] = jnp.zeros(points_s.shape, F32)
    for k, ref in enumerate((planck_ref, insol_ref, cond_ref)):
        points_s[k : k + 1, :gpoints] = ref[...]
    for r in range(rows):
        lit = mu_ref[r : r + 1, :] * daylight_ref[r].astype(F32)
        lit_s[r : r + 1, :] = rounded(lit)

    def column(k):
        line = jnp.broadcast_to(points_s[k : k + 1, :], (LANES, points_s.shape[1]))
        return jnp.transpose(line)[:padded]

    planck_s[...] = column(0).astype(BF)
    insol_s[...] = column(1).astype(BF)
    cond = column(2) * (-diffusivity * LOG2E)
    high = rounded(cond)
    lane = lax.broadcasted_iota(jnp.int32, (padded, LANES), 1)
    cond_s[...] = jnp.where(lane == 0, high, jnp.where(lane == 1, cond - high, 0.0)).astype(BF)
    inverse_s[...] = (1.0 / diffusivity) / rounded(mu_ref[...])

    def hats(l, _):
        after = jnp.minimum(l + 1, levels - 1)
        for g in range(groups):
            at = slice(g * ROWS, (g + 1) * ROWS)
            t = rounded(t_ref[l, at])
            t_pos = jnp.clip((t + 3.0) * ((NT - 1.0) / 6.0), 0.0, NT - 1.0)
            q_pos = jnp.clip(rounded(q_ref[l, at]) * (NQ - 1.0), 0.0, NQ - 1.0)
            for i in range(NT):
                th_s[g, l, i] = jnp.maximum(0.0, 1.0 - jnp.abs(t_pos - float(i)))
            for j in range(NQ):
                qh_s[g, l, j * ROWS : (j + 1) * ROWS] = jnp.maximum(
                    0.0, 1.0 - jnp.abs(q_pos - float(j))
                )
            dt_s[l, at] = 0.25 * (t - rounded(t_ref[after, at]))
        return 0

    unrolled(levels, 2, hats, 0)

    def spread(ref, index, row):
        return jnp.broadcast_to(ref[*index, pl.ds(row, 1), :], (ROWS, LANES))

    def wide(ref, index, row):
        one = spread(ref, index, row)
        return jnp.concatenate([one, one], axis=0).astype(BF)

    def weights(l, row):
        g, r = row // ROWS, row % ROWS
        qh = qh_s[g, l, pl.ds(r, NQ, stride=ROWS), :]
        qh = jnp.concatenate([qh, qh], axis=0).astype(BF)
        parts = []
        for m in range(NT // 2):
            pair = jnp.concatenate(
                [spread(th_s, (g, l, 2 * m), r), spread(th_s, (g, l, 2 * m + 1), r)], axis=0
            ).astype(BF)
            parts.append(pair * qh)
        cloud = wide(c_ref, (l,), row)
        return jnp.concatenate(parts + [cloud] * (NODES // 16), axis=0)

    def both(make):
        return jnp.concatenate([make(0), make(1)], axis=1)

    def tile(k):
        return slice(16 * k, 16 * k + 16)

    def put(ref, l, row, total):
        at = pl.ds(pl.multiple_of(row * ROWS, ROWS), ROWS)
        ref[l, at, :] = total[:ROWS] + total[ROWS:]

    def pair_of_rows(p, _):
        def transmit(l, _):
            rhs = both(lambda h: weights(l, 2 * p + h))
            lhs = jnp.concatenate([table_s[l], cond_s[...]], axis=1)
            depth = jnp.dot(lhs, rhs, preferred_element_type=F32)
            inverse = both(lambda h: wide(inverse_s, (), 2 * p + h))
            for k in range(tiles):
                part = depth[tile(k)].astype(BF)
                tr_s[l, tile(k)] = jnp.exp2(part)
                beam_s[l, tile(k)] = jnp.exp2(part * inverse)
            return 0

        unrolled(levels, 10, transmit, 0)

        for h in range(2):
            row = 2 * p + h
            lanes = slice(h * LANES, (h + 1) * LANES)

            def sweep(n, state):
                long, short, rising = (list(part) for part in state)
                m = levels - 1 - n
                step = wide(dt_s, (n,), row)
                up_step = wide(dt_s, (jnp.maximum(m - 1, 0),), row)
                down_total, up_total = 0.0, 0.0
                for k in range(0, tiles, 2):
                    down_part, up_part = 0.0, 0.0
                    for j in range(k, min(k + 2, tiles)):
                        planck = planck_s[tile(j)]
                        kept = tr_s[n, tile(j), lanes] * long[j]
                        short[j] = short[j] * beam_s[n, tile(j), lanes]
                        long[j] = kept + planck * step
                        risen = tr_s[m, tile(j), lanes] * rising[j]
                        rising[j] = risen + planck * up_step
                        down_part = kept + short[j] + down_part
                        up_part = risen + up_part
                    down_total = down_part.astype(F32) + down_total
                    up_total = up_part.astype(F32) + up_total
                put(down_s, n, row, down_total)
                put(up_s, m, row, up_total)
                return tuple(long), tuple(short), tuple(rising)

            start = wide(t_ref, (0,), row) * jnp.asarray(-0.25, BF) - jnp.asarray(1.0, BF)
            lit = wide(lit_s, (), row)
            state = (
                tuple(planck_s[tile(k)] * start for k in range(tiles)),
                tuple(insol_s[tile(k)] * lit for k in range(tiles)),
                (jnp.zeros((16, LANES), BF),) * tiles,
            )
            unrolled(levels, 6, sweep, state)
        return 0

    lax.fori_loop(0, pairs, pair_of_rows, 0)

    def total_of(k):
        return jnp.sum(rounded(points_s[k : k + 1, :]), axis=1, keepdims=True)

    planck_total, insol_total = total_of(0), total_of(1)

    def gathered(ref, l, g):
        base = g * ROWS * ROWS
        return sum(ref[l, pl.ds(base + k, ROWS, stride=ROWS), :] for k in range(ROWS))

    def source_of(l, g):
        return (1.0 + 0.25 * rounded(t_ref[l, g * ROWS : (g + 1) * ROWS])) * planck_total

    def finish(l, carry):
        after = jnp.minimum(l + 1, levels - 1)
        out = []
        for g in range(groups):
            down_in, up_out = carry[g]
            down_out = gathered(down_s, l, g) + source_of(l, g)
            up_in = source_of(after, g) - jnp.where(l == levels - 1, 0.0, gathered(up_s, after, g))
            heat_ref[l, g * ROWS : (g + 1) * ROWS] = (2.0 / gpoints) * (
                down_in - down_out + up_in - up_out
            )
            out.append((down_out, up_in))
        return tuple(out)

    begin = []
    for g in range(groups):
        lit = lit_s[g * ROWS : (g + 1) * ROWS]
        begin.append((lit * insol_total, source_of(0, g) - gathered(up_s, 0, g)))
    ends = unrolled(levels, 3, finish, tuple(begin))
    for g in range(groups):
        surface_s[g * ROWS : (g + 1) * ROWS] = ends[g][0] * (1.0 / gpoints)

    slots_ref[...] = jnp.zeros(slots_ref.shape, F32)

    def clear(h, _):
        taken_s[h] = 0
        return 0

    lax.fori_loop(0, slots_ref.shape[0] // capacity, clear, 0)

    def place(r, _):
        host = hosts_ref[r]
        k = taken_s[host]
        taken_s[host] = k + 1
        slots_ref[pl.ds(host * capacity + k, 1), :] = surface_s[pl.ds(r, 1), :]
        return 0

    lax.fori_loop(0, rows, place, 0)


VMEM_GRANT = 60 * 1024 * 1024


def radiate(hosts, daylight, host_count, capacity, t, q, c, mu, table, planck, insol, cond):
    levels, rows, width = t.shape
    gpoints = table.shape[1]
    padded = -(-gpoints // 16) * 16
    groups = rows // ROWS
    in_vmem = pl.BlockSpec(memory_space=pltpu.VMEM)
    two_rows = pltpu.VMEM((levels, padded, 2 * LANES), BF)
    per_tile = pltpu.VMEM((padded, LANES), BF)
    sums = pltpu.VMEM((levels, rows * ROWS, LANES), F32)
    return pl.pallas_call(
        functools.partial(column_kernel, gpoints, capacity),
        in_specs=[pl.BlockSpec(memory_space=pltpu.SMEM)] * 2 + [in_vmem] * 8,
        out_specs=[in_vmem, in_vmem],
        out_shape=[
            jax.ShapeDtypeStruct(t.shape, F32),
            jax.ShapeDtypeStruct((host_count * capacity, width), F32),
        ],
        scratch_shapes=[
            pltpu.VMEM((levels, padded, NODES), BF),
            per_tile,
            per_tile,
            per_tile,
            pltpu.VMEM((rows, width), F32),
            pltpu.VMEM((rows, width), F32),
            pltpu.VMEM((ROWS, -(-gpoints // LANES) * LANES), F32),
            pltpu.VMEM((groups, levels, NT, ROWS, LANES), F32),
            pltpu.VMEM((groups, levels, NQ * ROWS, LANES), F32),
            pltpu.VMEM((levels, rows, width), F32),
            two_rows,
            two_rows,
            sums,
            sums,
            pltpu.VMEM((rows, width), F32),
            pltpu.SMEM((host_count,), jnp.int32),
        ],
        compiler_params=pltpu.CompilerParams(vmem_limit_bytes=VMEM_GRANT),
        cost_estimate=pl.CostEstimate(
            flops=2 * levels * padded * 256 * rows * width,
            bytes_accessed=4 * 4 * levels * rows * width,
            transcendentals=2 * levels * padded * rows * width,
        ),
        name="columns",
    )(hosts, daylight, t, q, c, mu, table, planck[None], insol[None], cond[None])


def lines_of(levels):
    return -(-2 * levels // 32) * 32


def edge_kernel(t_ref, q_ref, out_ref):
    levels, rows, width = t_ref.shape
    lines = lines_of(levels)
    lane = lax.broadcasted_iota(jnp.int32, (rows, width), 1) // 2
    packed = jnp.zeros((rows, width), F32)
    for k, ref in enumerate((t_ref, q_ref)):
        for l in range(levels):
            n = k * levels + l
            v = ref[l]
            out_ref[n : n + 1, :] = v[:1]
            out_ref[lines + n : lines + n + 1, :] = v[rows - 1 :]
            packed = jnp.where(lane == n, pltpu.roll(v, 2 * n + 1, axis=1), packed)
    if lines > 2 * levels:
        rest = jnp.zeros((lines - 2 * levels, width), F32)
        out_ref[2 * levels : lines, :] = rest
        out_ref[lines + 2 * levels : 2 * lines, :] = rest
    out_ref[2 * lines :, :] = packed


def chunks(levels):
    count = max(n for n in range(1, 11) if levels % n == 0)
    return count, levels // count


def edges(t, q):
    levels, rows, width = t.shape
    return pl.pallas_call(
        edge_kernel,
        out_shape=jax.ShapeDtypeStruct((2 * lines_of(levels) + rows, width), F32),
        name="edges",
    )(t, q)


def stencil_kernel(
    levels, at_ref, t_ref, q_ref, heat_ref, west_ref, east_ref, south_ref, north_ref, t_out, q_out
):
    count, rows, width = t_ref.shape
    lane = lax.broadcasted_iota(jnp.int32, (rows, width), 1)
    row = lax.broadcasted_iota(jnp.int32, (rows, width), 0)

    def present(k, x):
        return jnp.where(at_ref[4 + k] != 0, x, 0.0)

    sides = jnp.where(
        lane % 2 == 0,
        present(1, pltpu.roll(east_ref[...], width - 1, axis=1)),
        present(0, pltpu.roll(west_ref[...], 1, axis=1)),
    )

    def smoothed(v, n):
        halo = pltpu.roll(sides, width - 1 - 2 * n, axis=1)
        west = jnp.where(lane == 0, halo, pltpu.roll(v, 1, axis=1))
        east = jnp.where(lane == width - 1, halo, pltpu.roll(v, width - 1, axis=1))
        below = present(2, south_ref[pl.ds(n, 1), :])
        above = present(3, north_ref[pl.ds(n, 1), :])
        south = jnp.where(row == 0, below, pltpu.roll(v, 1, axis=0))
        north = jnp.where(row == rows - 1, above, pltpu.roll(v, rows - 1, axis=0))
        return v + diffusion * (((north + south) + (east + west)) - 4.0 * v)

    for j in range(count):
        l = pl.program_id(0) * count + j
        t_out[j] = smoothed(t_ref[j], l) + heat_ref[j]
        q_out[j] = smoothed(q_ref[j], levels + l)


def diffuse(places, t, q, heating, packed):
    levels, rows, width = t.shape
    lines = lines_of(levels)
    count, steps = chunks(levels)
    block = pl.BlockSpec((count, rows, width), lambda i, at: (i, 0, 0))

    def part(which, height, place):
        return pl.BlockSpec((None, height, width), lambda i, at: (at[which], place, 0))

    out = jax.ShapeDtypeStruct(t.shape, F32)
    return pl.pallas_call(
        functools.partial(stencil_kernel, levels),
        grid_spec=pltpu.PrefetchScalarGridSpec(
            num_scalar_prefetch=1,
            grid=(steps,),
            in_specs=[
                block,
                block,
                block,
                part(0, rows, 2 * lines // rows),
                part(1, rows, 2 * lines // rows),
                part(2, lines, 1),
                part(3, lines, 0),
            ],
            out_specs=[block, block],
        ),
        out_shape=[out, out],
        cost_estimate=pl.CostEstimate(
            flops=200 * levels * rows * width * 8,
            bytes_accessed=5 * 4 * levels * rows * width,
            transcendentals=0,
        ),
        name="diffuse",
    )(places, t, q, heating, packed, packed, packed, packed)


def neighbour_places():
    x, y = lax.axis_index("gx"), lax.axis_index("gy")
    x_count, y_count = lax.axis_size("gx"), lax.axis_size("gy")
    places, exist = [], []
    for dx, dy in ((-1, 0), (1, 0), (0, -1), (0, 1)):
        there_x, there_y = x + dx, y + dy
        inside = jnp.logical_and(
            jnp.logical_and(there_x >= 0, there_x < x_count),
            jnp.logical_and(there_y >= 0, there_y < y_count),
        )
        places.append(jnp.where(inside, there_x * y_count + there_y, 0))
        exist.append(inside.astype(jnp.int32))
    return jnp.stack(places + exist).astype(jnp.int32)


def on_device(
    thermal_anomaly_grid,
    relative_moisture,
    overcast_share,
    sun_angle_projection,
    daylight_mask,
    radiator_owner_position,
    molecular_opacity_lookup,
    condensed_opacity_per_share,
    planck_emission_factor,
    insolation_quadrature_factor,
):
    host_count = lax.axis_size("gx")
    t, q = thermal_anomaly_grid, relative_moisture
    blocks = t.shape[1]
    capacity = max(2, (2 * blocks + host_count - 1) // host_count)

    packed = lax.all_gather(edges(t, q), ("gx", "gy"), axis=0)

    heating, sent = radiate(
        radiator_owner_position.reshape(blocks),
        daylight_mask.reshape(blocks),
        host_count,
        capacity,
        t,
        q,
        overcast_share,
        sun_angle_projection,
        molecular_opacity_lookup,
        planck_emission_factor,
        insolation_quadrature_factor,
        condensed_opacity_per_share,
    )
    slots = lax.all_to_all(
        sent.reshape(host_count, capacity, sent.shape[1]),
        "gx",
        split_axis=0,
        concat_axis=0,
        tiled=True,
    )
    t_next, q_next = diffuse(neighbour_places(), t, q, heating, packed)
    return t_next, q_next, slots[None, None]


def solution(mesh):
    placed = (
        P(None, "gy", "gx"),
        P(None, "gy", "gx"),
        P(None, "gy", "gx"),
        P("gy", "gx"),
        P("gx", "gy"),
        P("gx", "gy", None),
        P(),
        P(),
        P(),
        P(),
    )
    return jax.shard_map(
        on_device,
        mesh=mesh,
        in_specs=placed,
        out_specs=(P(None, "gy", "gx"), P(None, "gy", "gx"), P("gy", "gx", None, None, None)),
        check_vma=False,
    )
```

```python
import functools
import math

import jax
import jax.numpy as jnp
from jax import lax
from jax.experimental import pallas as pl
from jax.experimental.pallas import tpu as pltpu
from jax.sharding import PartitionSpec as P

NT = 16
NQ = 8
NODES = NT * NQ
LANES = 128
ROWS = 8

diffusion = 0.2
diffusivity = 1.66
LOG2E = math.log2(math.e)

BF = jnp.bfloat16
F32 = jnp.float32


def rounded(x):
    return x.astype(BF).astype(F32)


def unrolled(count, most, body, carry):
    steps = max(n for n in range(1, most + 1) if count % n == 0)

    def several(o, carry):
        for k in range(steps):
            carry = body(o * steps + k, carry)
        return carry

    return lax.fori_loop(0, count // steps, several, carry)


def column_kernel(
    gpoints,
    capacity,
    hosts_ref,
    daylight_ref,
    t_ref,
    q_ref,
    c_ref,
    mu_ref,
    table_ref,
    planck_ref,
    insol_ref,
    cond_ref,
    heat_ref,
    slots_ref,
    sides_ref,
    low_ref,
    high_ref,
    table_s,
    cond_s,
    planck_s,
    insol_s,
    inverse_s,
    lit_s,
    points_s,
    th_s,
    q_pos_s,
    dt_s,
    tr_s,
    beam_s,
    down_s,
    up_s,
    surface_s,
    taken_s,
):
    levels, rows, _ = t_ref.shape
    padded = table_s.shape[1]
    tiles = padded // 16
    groups = rows // ROWS
    pairs = rows // 2

    pack_edges(t_ref, q_ref, sides_ref, low_ref, high_ref)

    def prepare(l, _):
        layer = table_ref[l].astype(F32) * (-diffusivity * LOG2E)
        table_s[l] = jnp.concatenate(
            [layer, jnp.zeros((padded - gpoints, NODES), F32)], axis=0
        ).astype(BF)
        return 0

    unrolled(levels, 3, prepare, 0)

    points_s[...] = jnp.zeros(points_s.shape, F32)
    for k, ref in enumerate((planck_ref, insol_ref, cond_ref)):
        points_s[k : k + 1, :gpoints] = ref[...]
    for r in range(rows):
        lit = mu_ref[r : r + 1, :] * daylight_ref[r].astype(F32)
        lit_s[r : r + 1, :] = rounded(lit)

    def column(k):
        line = jnp.broadcast_to(points_s[k : k + 1, :], (LANES, points_s.shape[1]))
        return jnp.transpose(line)[:padded]

    planck_s[...] = column(0).astype(BF)
    insol_s[...] = column(1).astype(BF)
    cond_s[...] = (column(2) * (-diffusivity * LOG2E)).astype(BF)
    inverse_s[...] = (1.0 / diffusivity) / rounded(mu_ref[...])

    def hats(l, _):
        after = jnp.minimum(l + 1, levels - 1)
        for g in range(groups):
            at = slice(g * ROWS, (g + 1) * ROWS)
            t = rounded(t_ref[l, at])
            t_pos = jnp.clip((t + 3.0) * ((NT - 1.0) / 6.0), 0.0, NT - 1.0)
            q_pos = jnp.clip(rounded(q_ref[l, at]) * (NQ - 1.0), 0.0, NQ - 1.0)
            for i in range(NT):
                th_s[g, l, i] = jnp.maximum(0.0, 1.0 - jnp.abs(t_pos - float(i)))
            q_pos_s[l, at] = q_pos
            dt_s[l, at] = 0.25 * (t - rounded(t_ref[after, at]))
        return 0

    unrolled(levels, 2, hats, 0)

    def spread(ref, index, row):
        return jnp.broadcast_to(ref[*index, pl.ds(row, 1), :], (ROWS, LANES))

    def wide(ref, index, row):
        one = spread(ref, index, row)
        return jnp.concatenate([one, one], axis=0).astype(BF)

    def weights(l, row):
        g, r = row // ROWS, row % ROWS
        node = lax.broadcasted_iota(jnp.int32, (NQ, LANES), 0).astype(F32)
        qh = jnp.maximum(0.0, 1.0 - jnp.abs(spread(q_pos_s, (l,), row) - node))
        qh = jnp.concatenate([qh, qh], axis=0).astype(BF)
        parts = []
        for m in range(NT // 2):
            pair = jnp.concatenate(
                [spread(th_s, (g, l, 2 * m), r), spread(th_s, (g, l, 2 * m + 1), r)], axis=0
            ).astype(BF)
            parts.append(pair * qh)
        return jnp.concatenate(parts, axis=0)

    def both(make):
        return jnp.concatenate([make(0), make(1)], axis=1)

    def tile(k):
        return slice(16 * k, 16 * k + 16)

    def put(ref, l, row, total):
        at = pl.ds(pl.multiple_of(row * ROWS, ROWS), ROWS)
        ref[l, at, :] = total[:ROWS] + total[ROWS:]

    def pair_of_rows(p, _):
        def transmit(l, _):
            rhs = both(lambda h: weights(l, 2 * p + h))
            depth = jnp.dot(table_s[l], rhs, preferred_element_type=F32)
            cloud = both(lambda h: wide(c_ref, (l,), 2 * p + h))
            inverse = both(lambda h: wide(inverse_s, (), 2 * p + h))
            for k in range(tiles):
                cond = cond_s[tile(k)]
                part = depth[tile(k)].astype(BF) + jnp.concatenate([cond, cond], axis=1) * cloud
                tr_s[l, tile(k)] = jnp.exp2(part)
                beam_s[l, tile(k)] = jnp.exp2(part * inverse)
            return 0

        unrolled(levels, 30, transmit, 0)

        for h in range(2):
            row = 2 * p + h
            lanes = slice(h * LANES, (h + 1) * LANES)

            def sweep(n, state):
                long, short, rising = (list(part) for part in state)
                m = levels - 1 - n
                step = wide(dt_s, (n,), row)
                up_step = wide(dt_s, (jnp.maximum(m - 1, 0),), row)
                down_total, up_total = 0.0, 0.0
                for k in range(0, tiles, 3):
                    down_part, up_part = 0.0, 0.0
                    for j in range(k, min(k + 3, tiles)):
                        planck = planck_s[tile(j)]
                        kept = tr_s[n, tile(j), lanes] * long[j]
                        short[j] = short[j] * beam_s[n, tile(j), lanes]
                        long[j] = kept + planck * step
                        risen = tr_s[m, tile(j), lanes] * rising[j]
                        rising[j] = risen + planck * up_step
                        down_part = kept + short[j] + down_part
                        up_part = risen + up_part
                    down_total = down_part.astype(F32) + down_total
                    up_total = up_part.astype(F32) + up_total
                put(down_s, n, row, down_total)
                put(up_s, m, row, up_total)
                return tuple(long), tuple(short), tuple(rising)

            start = wide(t_ref, (0,), row) * jnp.asarray(-0.25, BF) - jnp.asarray(1.0, BF)
            lit = wide(lit_s, (), row)
            state = (
                tuple(planck_s[tile(k)] * start for k in range(tiles)),
                tuple(insol_s[tile(k)] * lit for k in range(tiles)),
                (jnp.zeros((16, LANES), BF),) * tiles,
            )
            unrolled(levels, 15, sweep, state)
        return 0

    lax.fori_loop(0, pairs, pair_of_rows, 0)

    def total_of(k):
        return jnp.sum(rounded(points_s[k : k + 1, :]), axis=1, keepdims=True)

    planck_total, insol_total = total_of(0), total_of(1)

    def gathered(ref, l, g):
        base = g * ROWS * ROWS
        return sum(ref[l, pl.ds(base + k, ROWS, stride=ROWS), :] for k in range(ROWS))

    def source_of(l, g):
        return (1.0 + 0.25 * rounded(t_ref[l, g * ROWS : (g + 1) * ROWS])) * planck_total

    def finish(l, carry):
        after = jnp.minimum(l + 1, levels - 1)
        out = []
        for g in range(groups):
            down_in, up_out = carry[g]
            down_out = gathered(down_s, l, g) + source_of(l, g)
            up_in = source_of(after, g) - jnp.where(l == levels - 1, 0.0, gathered(up_s, after, g))
            heat_ref[l, g * ROWS : (g + 1) * ROWS] = (2.0 / gpoints) * (
                down_in - down_out + up_in - up_out
            )
            out.append((down_out, up_in))
        return tuple(out)

    begin = []
    for g in range(groups):
        lit = lit_s[g * ROWS : (g + 1) * ROWS]
        begin.append((lit * insol_total, source_of(0, g) - gathered(up_s, 0, g)))
    ends = unrolled(levels, 3, finish, tuple(begin))
    for g in range(groups):
        surface_s[g * ROWS : (g + 1) * ROWS] = ends[g][0] * (1.0 / gpoints)

    slots_ref[...] = jnp.zeros(slots_ref.shape, F32)

    def clear(h, _):
        taken_s[h] = 0
        return 0

    lax.fori_loop(0, slots_ref.shape[0] // capacity, clear, 0)

    def place(r, _):
        host = hosts_ref[r]
        k = taken_s[host]
        taken_s[host] = k + 1
        slots_ref[pl.ds(host * capacity + k, 1), :] = surface_s[pl.ds(r, 1), :]
        return 0

    lax.fori_loop(0, rows, place, 0)


def pack_edges(t_ref, q_ref, sides_ref, low_ref, high_ref):
    levels, rows, width = t_ref.shape
    lane = lax.broadcasted_iota(jnp.int32, (rows, width), 1) // 2

    def body(l, packed):
        for k, ref in enumerate((t_ref, q_ref)):
            n = k * levels + l
            v = ref[l]
            low_ref[pl.ds(n, 1), :] = v[:1]
            high_ref[pl.ds(n, 1), :] = v[rows - 1 :]
            packed = jnp.where(lane == n, pltpu.roll(v, 2 * n + 1, axis=1), packed)
        return packed

    sides_ref[...] = unrolled(levels, 6, body, jnp.zeros((rows, width), F32))


VMEM_GRANT = 60 * 1024 * 1024


def radiate(hosts, daylight, host_count, capacity, t, q, c, mu, table, planck, insol, cond):
    levels, rows, width = t.shape
    gpoints = table.shape[1]
    padded = -(-gpoints // 16) * 16
    groups = rows // ROWS
    in_vmem = pl.BlockSpec(memory_space=pltpu.VMEM)
    two_rows = pltpu.VMEM((levels, padded, 2 * LANES), BF)
    per_tile = pltpu.VMEM((padded, LANES), BF)
    sums = pltpu.VMEM((levels, rows * ROWS, LANES), F32)
    return pl.pallas_call(
        functools.partial(column_kernel, gpoints, capacity),
        in_specs=[pl.BlockSpec(memory_space=pltpu.SMEM)] * 2 + [in_vmem] * 8,
        out_specs=[in_vmem] * 5,
        out_shape=[
            jax.ShapeDtypeStruct(t.shape, F32),
            jax.ShapeDtypeStruct((host_count * capacity, width), F32),
            jax.ShapeDtypeStruct((rows, width), F32),
            jax.ShapeDtypeStruct((2 * levels, width), F32),
            jax.ShapeDtypeStruct((2 * levels, width), F32),
        ],
        scratch_shapes=[
            pltpu.VMEM((levels, padded, NODES), BF),
            per_tile,
            per_tile,
            per_tile,
            pltpu.VMEM((rows, width), F32),
            pltpu.VMEM((rows, width), F32),
            pltpu.VMEM((ROWS, -(-gpoints // LANES) * LANES), F32),
            pltpu.VMEM((groups, levels, NT, ROWS, LANES), F32),
            pltpu.VMEM((levels, rows, width), F32),
            pltpu.VMEM((levels, rows, width), F32),
            two_rows,
            two_rows,
            sums,
            sums,
            pltpu.VMEM((rows, width), F32),
            pltpu.SMEM((host_count,), jnp.int32),
        ],
        compiler_params=pltpu.CompilerParams(vmem_limit_bytes=VMEM_GRANT),
        cost_estimate=pl.CostEstimate(
            flops=2 * levels * padded * 256 * rows * width,
            bytes_accessed=4 * 4 * levels * rows * width,
            transcendentals=2 * levels * padded * rows * width,
        ),
        name="columns",
    )(hosts, daylight, t, q, c, mu, table, planck[None], insol[None], cond[None])


def chunks(levels):
    count = max(n for n in range(1, 11) if levels % n == 0)
    return count, levels // count


def stencil_kernel(
    levels, t_ref, q_ref, heat_ref, west_ref, east_ref, south_ref, north_ref, t_out, q_out
):
    count, rows, width = t_ref.shape
    lane = lax.broadcasted_iota(jnp.int32, (rows, width), 1)
    row = lax.broadcasted_iota(jnp.int32, (rows, width), 0)

    sides = jnp.where(
        lane % 2 == 0,
        pltpu.roll(east_ref[...], width - 1, axis=1),
        pltpu.roll(west_ref[...], 1, axis=1),
    )

    def smoothed(v, n):
        halo = pltpu.roll(sides, width - 1 - 2 * n, axis=1)
        west = jnp.where(lane == 0, halo, pltpu.roll(v, 1, axis=1))
        east = jnp.where(lane == width - 1, halo, pltpu.roll(v, width - 1, axis=1))
        south = jnp.where(row == 0, south_ref[pl.ds(n, 1), :], pltpu.roll(v, 1, axis=0))
        north = jnp.where(row == rows - 1, north_ref[pl.ds(n, 1), :], pltpu.roll(v, rows - 1, axis=0))
        return v + diffusion * (((north + south) + (east + west)) - 4.0 * v)

    for j in range(count):
        l = pl.program_id(0) * count + j
        t_out[j] = smoothed(t_ref[j], l) + heat_ref[j]
        q_out[j] = smoothed(q_ref[j], levels + l)


def diffuse(t, q, heating, west, east, south, north):
    levels, rows, width = t.shape
    count, steps = chunks(levels)
    block = pl.BlockSpec((count, rows, width), lambda i: (i, 0, 0))

    def whole(x):
        return pl.BlockSpec(x.shape, lambda i: (0, 0))

    out = jax.ShapeDtypeStruct(t.shape, F32)
    return pl.pallas_call(
        functools.partial(stencil_kernel, levels),
        grid=(steps,),
        in_specs=[block, block, block, whole(west), whole(east), whole(south), whole(north)],
        out_specs=[block, block],
        out_shape=[out, out],
        cost_estimate=pl.CostEstimate(
            flops=200 * levels * rows * width * 8,
            bytes_accessed=5 * 4 * levels * rows * width,
            transcendentals=0,
        ),
        name="diffuse",
    )(t, q, heating, west, east, south, north)


def neighbours(low_edge, high_edge, axis):
    count = lax.axis_size(axis)
    forward = [(i, i + 1) for i in range(count - 1)]
    backward = [(target, source) for source, target in forward]
    return lax.ppermute(high_edge, axis, forward), lax.ppermute(low_edge, axis, backward)


def on_device(
    thermal_anomaly_grid,
    relative_moisture,
    overcast_share,
    sun_angle_projection,
    daylight_mask,
    radiator_owner_position,
    molecular_opacity_lookup,
    condensed_opacity_per_share,
    planck_emission_factor,
    insolation_quadrature_factor,
):
    host_count = lax.axis_size("gx")
    t, q = thermal_anomaly_grid, relative_moisture
    blocks = t.shape[1]
    capacity = max(2, (2 * blocks + host_count - 1) // host_count)

    heating, sent, sides, low, high = radiate(
        radiator_owner_position.reshape(blocks),
        daylight_mask.reshape(blocks),
        host_count,
        capacity,
        t,
        q,
        overcast_share,
        sun_angle_projection,
        molecular_opacity_lookup,
        planck_emission_factor,
        insolation_quadrature_factor,
        condensed_opacity_per_share,
    )
    slots = lax.all_to_all(
        sent.reshape(host_count, capacity, sent.shape[1]),
        "gx",
        split_axis=0,
        concat_axis=0,
        tiled=True,
    )
    west, east = neighbours(sides, sides, "gx")
    south, north = neighbours(low, high, "gy")
    t_next, q_next = diffuse(t, q, heating, west, east, south, north)
    return t_next, q_next, slots[None, None]


def solution(mesh):
    placed = (
        P(None, "gy", "gx"),
        P(None, "gy", "gx"),
        P(None, "gy", "gx"),
        P("gy", "gx"),
        P("gx", "gy"),
        P("gx", "gy", None),
        P(),
        P(),
        P(),
        P(),
    )
    return jax.shard_map(
        on_device,
        mesh=mesh,
        in_specs=placed,
        out_specs=(P(None, "gy", "gx"), P(None, "gy", "gx"), P("gy", "gx", None, None, None)),
        check_vma=False,
    )
```

```python
import functools
import math

import jax
import jax.numpy as jnp
from jax import lax
from jax.experimental import pallas as pl
from jax.experimental.pallas import tpu as pltpu
from jax.sharding import PartitionSpec as P

NT = 16
NQ = 8
NODES = NT * NQ
LANES = 128
ROWS = 8

diffusion = 0.2
diffusivity = 1.66
LAG = 1
LOG2E = math.log2(math.e)

BF = jnp.bfloat16
F32 = jnp.float32


def rounded(x):
    return x.astype(BF).astype(F32)


def unrolled(count, most, body, carry):
    steps = max(n for n in range(1, most + 1) if count % n == 0)

    def several(o, carry):
        for k in range(steps):
            carry = body(o * steps + k, carry)
        return carry

    return lax.fori_loop(0, count // steps, several, carry)


def column_kernel(
    gpoints,
    capacity,
    hosts_ref,
    daylight_ref,
    t_ref,
    q_ref,
    c_ref,
    mu_ref,
    table_ref,
    planck_ref,
    insol_ref,
    cond_ref,
    heat_ref,
    slots_ref,
    sides_ref,
    low_ref,
    high_ref,
    table_s,
    cond_s,
    planck_s,
    insol_s,
    inverse_s,
    lit_s,
    points_s,
    th_s,
    q_pos_s,
    dt_s,
    tr_s,
    beam_s,
    down_s,
    up_s,
    surface_s,
    taken_s,
):
    levels, rows, _ = t_ref.shape
    padded = table_s.shape[1]
    tiles = padded // 16
    groups = rows // ROWS
    pairs = rows // 2

    pack_edges(t_ref, q_ref, sides_ref, low_ref, high_ref)

    def prepare(l, _):
        layer = table_ref[l].astype(F32) * (-diffusivity * LOG2E)
        table_s[l] = jnp.concatenate(
            [layer, jnp.zeros((padded - gpoints, NODES), F32)], axis=0
        ).astype(BF)
        return 0

    unrolled(levels, 3, prepare, 0)

    points_s[...] = jnp.zeros(points_s.shape, F32)
    for k, ref in enumerate((planck_ref, insol_ref, cond_ref)):
        points_s[k : k + 1, :gpoints] = ref[...]
    for r in range(rows):
        lit = mu_ref[r : r + 1, :] * daylight_ref[r].astype(F32)
        lit_s[r : r + 1, :] = rounded(lit)

    def column(k):
        line = jnp.broadcast_to(points_s[k : k + 1, :], (LANES, points_s.shape[1]))
        return jnp.transpose(line)[:padded]

    planck_s[...] = column(0).astype(BF)
    insol_s[...] = column(1).astype(BF)
    cond_s[...] = (column(2) * (-diffusivity * LOG2E)).astype(BF)
    inverse_s[...] = (1.0 / diffusivity) / rounded(mu_ref[...])

    def hats(l, _):
        after = jnp.minimum(l + 1, levels - 1)
        for g in range(groups):
            at = slice(g * ROWS, (g + 1) * ROWS)
            t = rounded(t_ref[l, at])
            t_pos = jnp.clip((t + 3.0) * ((NT - 1.0) / 6.0), 0.0, NT - 1.0)
            q_pos = jnp.clip(rounded(q_ref[l, at]) * (NQ - 1.0), 0.0, NQ - 1.0)
            for i in range(NT):
                th_s[g, l, i] = jnp.maximum(0.0, 1.0 - jnp.abs(t_pos - float(i)))
            q_pos_s[l, at] = q_pos
            dt_s[l, at] = 0.25 * (t - rounded(t_ref[after, at]))
        return 0

    unrolled(levels, 2, hats, 0)

    def spread(ref, index, row):
        return jnp.broadcast_to(ref[*index, pl.ds(row, 1), :], (ROWS, LANES))

    def wide(ref, index, row):
        one = spread(ref, index, row)
        return jnp.concatenate([one, one], axis=0).astype(BF)

    def weights(l, row):
        g, r = row // ROWS, row % ROWS
        node = lax.broadcasted_iota(jnp.int32, (NQ, LANES), 0).astype(F32)
        qh = jnp.maximum(0.0, 1.0 - jnp.abs(spread(q_pos_s, (l,), row) - node))
        qh = jnp.concatenate([qh, qh], axis=0).astype(BF)
        parts = []
        for m in range(NT // 2):
            pair = jnp.concatenate(
                [spread(th_s, (g, l, 2 * m), r), spread(th_s, (g, l, 2 * m + 1), r)], axis=0
            ).astype(BF)
            parts.append(pair * qh)
        return jnp.concatenate(parts, axis=0)

    def both(make):
        return jnp.concatenate([make(0), make(1)], axis=1)

    def tile(k):
        return slice(16 * k, 16 * k + 16)

    def put(ref, l, row, total):
        at = pl.ds(pl.multiple_of(row * ROWS, ROWS), ROWS)
        ref[l, at, :] = total[:ROWS] + total[ROWS:]

    def pair_of_rows(p, _):
        def transmit(l, _):
            rhs = both(lambda h: weights(l, 2 * p + h))
            depth = jnp.dot(table_s[l], rhs, preferred_element_type=F32)
            cloud = both(lambda h: wide(c_ref, (l,), 2 * p + h))
            inverse = both(lambda h: wide(inverse_s, (), 2 * p + h))
            for k in range(tiles):
                cond = cond_s[tile(k)]
                part = depth[tile(k)].astype(BF) + jnp.concatenate([cond, cond], axis=1) * cloud
                tr_s[l, tile(k)] = jnp.exp2(part)
                beam_s[l, tile(k)] = jnp.exp2(part * inverse)
            return 0

        def sweeps(h):
            row = 2 * p + h
            lanes = slice(h * LANES, (h + 1) * LANES)

            def sweep(n, state):
                long, short, rising = (list(part) for part in state)
                m = levels - 1 - n
                step = wide(dt_s, (n,), row)
                up_step = wide(dt_s, (max(m - 1, 0),), row)
                down_total, up_total = 0.0, 0.0
                for k in range(0, tiles, 3):
                    down_part, up_part = 0.0, 0.0
                    for j in range(k, min(k + 3, tiles)):
                        planck = planck_s[tile(j)]
                        kept = tr_s[n, tile(j), lanes] * long[j]
                        short[j] = short[j] * beam_s[n, tile(j), lanes]
                        long[j] = kept + planck * step
                        risen = tr_s[m, tile(j), lanes] * rising[j]
                        rising[j] = risen + planck * up_step
                        down_part = kept + short[j] + down_part
                        up_part = risen + up_part
                    down_total = down_part.astype(F32) + down_total
                    up_total = up_part.astype(F32) + up_total
                put(down_s, n, row, down_total)
                put(up_s, m, row, up_total)
                return tuple(long), tuple(short), tuple(rising)

            start = wide(t_ref, (0,), row) * jnp.asarray(-0.25, BF) - jnp.asarray(1.0, BF)
            lit = wide(lit_s, (), row)
            state = (
                tuple(planck_s[tile(k)] * start for k in range(tiles)),
                tuple(insol_s[tile(k)] * lit for k in range(tiles)),
                (jnp.zeros((16, LANES), BF),) * tiles,
            )
            return sweep, state

        sweep, state = sweeps(0)
        half = (levels + 1) // 2
        for n in range(half + LAG):
            if n < half:
                transmit(n, 0)
                if levels - 1 - n != n:
                    transmit(levels - 1 - n, 0)
            if n >= LAG:
                state = sweep(n - LAG, state)
        for n in range(half, levels):
            state = sweep(n, state)
        sweep, state = sweeps(1)
        for n in range(levels):
            state = sweep(n, state)
        return 0

    lax.fori_loop(0, pairs, pair_of_rows, 0)

    def total_of(k):
        return jnp.sum(rounded(points_s[k : k + 1, :]), axis=1, keepdims=True)

    planck_total, insol_total = total_of(0), total_of(1)

    def gathered(ref, l, g):
        base = g * ROWS * ROWS
        return sum(ref[l, pl.ds(base + k, ROWS, stride=ROWS), :] for k in range(ROWS))

    def source_of(l, g):
        return (1.0 + 0.25 * rounded(t_ref[l, g * ROWS : (g + 1) * ROWS])) * planck_total

    def finish(l, carry):
        after = jnp.minimum(l + 1, levels - 1)
        out = []
        for g in range(groups):
            down_in, up_out = carry[g]
            down_out = gathered(down_s, l, g) + source_of(l, g)
            up_in = source_of(after, g) - jnp.where(l == levels - 1, 0.0, gathered(up_s, after, g))
            heat_ref[l, g * ROWS : (g + 1) * ROWS] = (2.0 / gpoints) * (
                down_in - down_out + up_in - up_out
            )
            out.append((down_out, up_in))
        return tuple(out)

    begin = []
    for g in range(groups):
        lit = lit_s[g * ROWS : (g + 1) * ROWS]
        begin.append((lit * insol_total, source_of(0, g) - gathered(up_s, 0, g)))
    ends = unrolled(levels, 3, finish, tuple(begin))
    for g in range(groups):
        surface_s[g * ROWS : (g + 1) * ROWS] = ends[g][0] * (1.0 / gpoints)

    slots_ref[...] = jnp.zeros(slots_ref.shape, F32)

    def clear(h, _):
        taken_s[h] = 0
        return 0

    lax.fori_loop(0, slots_ref.shape[0] // capacity, clear, 0)

    def place(r, _):
        host = hosts_ref[r]
        k = taken_s[host]
        taken_s[host] = k + 1
        slots_ref[pl.ds(host * capacity + k, 1), :] = surface_s[pl.ds(r, 1), :]
        return 0

    lax.fori_loop(0, rows, place, 0)


def pack_edges(t_ref, q_ref, sides_ref, low_ref, high_ref):
    levels, rows, width = t_ref.shape
    lane = lax.broadcasted_iota(jnp.int32, (rows, width), 1) // 2

    def body(l, packed):
        for k, ref in enumerate((t_ref, q_ref)):
            n = k * levels + l
            v = ref[l]
            low_ref[pl.ds(n, 1), :] = v[:1]
            high_ref[pl.ds(n, 1), :] = v[rows - 1 :]
            packed = jnp.where(lane == n, pltpu.roll(v, 2 * n + 1, axis=1), packed)
        return packed

    sides_ref[...] = unrolled(levels, 6, body, jnp.zeros((rows, width), F32))


VMEM_GRANT = 60 * 1024 * 1024


def radiate(hosts, daylight, host_count, capacity, t, q, c, mu, table, planck, insol, cond):
    levels, rows, width = t.shape
    gpoints = table.shape[1]
    padded = -(-gpoints // 16) * 16
    groups = rows // ROWS
    in_vmem = pl.BlockSpec(memory_space=pltpu.VMEM)
    two_rows = pltpu.VMEM((levels, padded, 2 * LANES), BF)
    per_tile = pltpu.VMEM((padded, LANES), BF)
    sums = pltpu.VMEM((levels, rows * ROWS, LANES), F32)
    return pl.pallas_call(
        functools.partial(column_kernel, gpoints, capacity),
        in_specs=[pl.BlockSpec(memory_space=pltpu.SMEM)] * 2 + [in_vmem] * 8,
        out_specs=[in_vmem] * 5,
        out_shape=[
            jax.ShapeDtypeStruct(t.shape, F32),
            jax.ShapeDtypeStruct((host_count * capacity, width), F32),
            jax.ShapeDtypeStruct((rows, width), F32),
            jax.ShapeDtypeStruct((2 * levels, width), F32),
            jax.ShapeDtypeStruct((2 * levels, width), F32),
        ],
        scratch_shapes=[
            pltpu.VMEM((levels, padded, NODES), BF),
            per_tile,
            per_tile,
            per_tile,
            pltpu.VMEM((rows, width), F32),
            pltpu.VMEM((rows, width), F32),
            pltpu.VMEM((ROWS, -(-gpoints // LANES) * LANES), F32),
            pltpu.VMEM((groups, levels, NT, ROWS, LANES), F32),
            pltpu.VMEM((levels, rows, width), F32),
            pltpu.VMEM((levels, rows, width), F32),
            two_rows,
            two_rows,
            sums,
            sums,
            pltpu.VMEM((rows, width), F32),
            pltpu.SMEM((host_count,), jnp.int32),
        ],
        compiler_params=pltpu.CompilerParams(vmem_limit_bytes=VMEM_GRANT),
        cost_estimate=pl.CostEstimate(
            flops=2 * levels * padded * 256 * rows * width,
            bytes_accessed=4 * 4 * levels * rows * width,
            transcendentals=2 * levels * padded * rows * width,
        ),
        name="columns",
    )(hosts, daylight, t, q, c, mu, table, planck[None], insol[None], cond[None])


def chunks(levels):
    count = max(n for n in range(1, 11) if levels % n == 0)
    return count, levels // count


def stencil_kernel(
    levels, t_ref, q_ref, heat_ref, west_ref, east_ref, south_ref, north_ref, t_out, q_out
):
    count, rows, width = t_ref.shape
    lane = lax.broadcasted_iota(jnp.int32, (rows, width), 1)
    row = lax.broadcasted_iota(jnp.int32, (rows, width), 0)

    sides = jnp.where(
        lane % 2 == 0,
        pltpu.roll(east_ref[...], width - 1, axis=1),
        pltpu.roll(west_ref[...], 1, axis=1),
    )

    def smoothed(v, n):
        halo = pltpu.roll(sides, width - 1 - 2 * n, axis=1)
        west = jnp.where(lane == 0, halo, pltpu.roll(v, 1, axis=1))
        east = jnp.where(lane == width - 1, halo, pltpu.roll(v, width - 1, axis=1))
        south = jnp.where(row == 0, south_ref[pl.ds(n, 1), :], pltpu.roll(v, 1, axis=0))
        north = jnp.where(row == rows - 1, north_ref[pl.ds(n, 1), :], pltpu.roll(v, rows - 1, axis=0))
        return v + diffusion * (((north + south) + (east + west)) - 4.0 * v)

    for j in range(count):
        l = pl.program_id(0) * count + j
        t_out[j] = smoothed(t_ref[j], l) + heat_ref[j]
        q_out[j] = smoothed(q_ref[j], levels + l)


def diffuse(t, q, heating, west, east, south, north):
    levels, rows, width = t.shape
    count, steps = chunks(levels)
    block = pl.BlockSpec((count, rows, width), lambda i: (i, 0, 0))

    def whole(x):
        return pl.BlockSpec(x.shape, lambda i: (0, 0))

    out = jax.ShapeDtypeStruct(t.shape, F32)
    return pl.pallas_call(
        functools.partial(stencil_kernel, levels),
        grid=(steps,),
        in_specs=[block, block, block, whole(west), whole(east), whole(south), whole(north)],
        out_specs=[block, block],
        out_shape=[out, out],
        cost_estimate=pl.CostEstimate(
            flops=200 * levels * rows * width * 8,
            bytes_accessed=5 * 4 * levels * rows * width,
            transcendentals=0,
        ),
        name="diffuse",
    )(t, q, heating, west, east, south, north)


def neighbours(low_edge, high_edge, axis):
    count = lax.axis_size(axis)
    forward = [(i, i + 1) for i in range(count - 1)]
    backward = [(target, source) for source, target in forward]
    return lax.ppermute(high_edge, axis, forward), lax.ppermute(low_edge, axis, backward)


def on_device(
    thermal_anomaly_grid,
    relative_moisture,
    overcast_share,
    sun_angle_projection,
    daylight_mask,
    radiator_owner_position,
    molecular_opacity_lookup,
    condensed_opacity_per_share,
    planck_emission_factor,
    insolation_quadrature_factor,
):
    host_count = lax.axis_size("gx")
    t, q = thermal_anomaly_grid, relative_moisture
    blocks = t.shape[1]
    capacity = max(2, (2 * blocks + host_count - 1) // host_count)

    heating, sent, sides, low, high = radiate(
        radiator_owner_position.reshape(blocks),
        daylight_mask.reshape(blocks),
        host_count,
        capacity,
        t,
        q,
        overcast_share,
        sun_angle_projection,
        molecular_opacity_lookup,
        planck_emission_factor,
        insolation_quadrature_factor,
        condensed_opacity_per_share,
    )
    slots = lax.all_to_all(
        sent.reshape(host_count, capacity, sent.shape[1]),
        "gx",
        split_axis=0,
        concat_axis=0,
        tiled=True,
    )
    west, east = neighbours(sides, sides, "gx")
    south, north = neighbours(low, high, "gy")
    t_next, q_next = diffuse(t, q, heating, west, east, south, north)
    return t_next, q_next, slots[None, None]


def solution(mesh):
    placed = (
        P(None, "gy", "gx"),
        P(None, "gy", "gx"),
        P(None, "gy", "gx"),
        P("gy", "gx"),
        P("gx", "gy"),
        P("gx", "gy", None),
        P(),
        P(),
        P(),
        P(),
    )
    return jax.shard_map(
        on_device,
        mesh=mesh,
        in_specs=placed,
        out_specs=(P(None, "gy", "gx"), P(None, "gy", "gx"), P("gy", "gx", None, None, None)),
        check_vma=False,
    )
```

```python
import functools
import math

import jax
import jax.numpy as jnp
from jax import lax
from jax.experimental import pallas as pl
from jax.experimental.pallas import tpu as pltpu
from jax.sharding import PartitionSpec as P

NT = 16
NQ = 8
NODES = NT * NQ
LANES = 128
ROWS = 8

diffusion = 0.2
diffusivity = 1.66
LOG2E = math.log2(math.e)

BF = jnp.bfloat16
F32 = jnp.float32


def rounded(x):
    return x.astype(BF).astype(F32)


def unrolled(count, most, body, carry):
    steps = max(n for n in range(1, most + 1) if count % n == 0)

    def several(o, carry):
        for k in range(steps):
            carry = body(o * steps + k, carry)
        return carry

    return lax.fori_loop(0, count // steps, several, carry)


def column_kernel(
    gpoints,
    capacity,
    hosts_ref,
    daylight_ref,
    t_ref,
    q_ref,
    c_ref,
    mu_ref,
    table_ref,
    planck_ref,
    insol_ref,
    cond_ref,
    heat_ref,
    slots_ref,
    sides_ref,
    low_ref,
    high_ref,
    table_s,
    cond_s,
    planck_s,
    insol_s,
    inverse_s,
    lit_s,
    points_s,
    th_s,
    q_pos_s,
    dt_s,
    tr_s,
    beam_s,
    down_s,
    up_s,
    surface_s,
    taken_s,
):
    levels, rows, _ = t_ref.shape
    padded = table_s.shape[1]
    tiles = padded // 16
    groups = rows // ROWS
    pairs = rows // 2

    pack_edges(t_ref, q_ref, sides_ref, low_ref, high_ref)

    def prepare(l, _):
        layer = table_ref[l].astype(F32) * (-diffusivity * LOG2E)
        table_s[l] = jnp.concatenate(
            [layer, jnp.zeros((padded - gpoints, NODES), F32)], axis=0
        ).astype(BF)
        return 0

    unrolled(levels, 3, prepare, 0)

    points_s[...] = jnp.zeros(points_s.shape, F32)
    for k, ref in enumerate((planck_ref, insol_ref, cond_ref)):
        points_s[k : k + 1, :gpoints] = ref[...]
    for r in range(rows):
        lit = mu_ref[r : r + 1, :] * daylight_ref[r].astype(F32)
        lit_s[r : r + 1, :] = rounded(lit)

    def column(k):
        line = jnp.broadcast_to(points_s[k : k + 1, :], (LANES, points_s.shape[1]))
        return jnp.transpose(line)[:padded]

    planck_s[...] = column(0).astype(BF)
    insol_s[...] = column(1).astype(BF)
    cond_s[...] = (column(2) * (-diffusivity * LOG2E)).astype(BF)
    inverse_s[...] = (1.0 / diffusivity) / rounded(mu_ref[...])

    def hats(l, _):
        after = jnp.minimum(l + 1, levels - 1)
        for g in range(groups):
            at = slice(g * ROWS, (g + 1) * ROWS)
            t = rounded(t_ref[l, at])
            t_pos = jnp.clip((t + 3.0) * ((NT - 1.0) / 6.0), 0.0, NT - 1.0)
            q_pos = jnp.clip(rounded(q_ref[l, at]) * (NQ - 1.0), 0.0, NQ - 1.0)
            for i in range(NT):
                th_s[g, l, i] = jnp.maximum(0.0, 1.0 - jnp.abs(t_pos - float(i)))
            q_pos_s[l, at] = q_pos
            dt_s[l, at] = 0.25 * (t - rounded(t_ref[after, at]))
        return 0

    unrolled(levels, 2, hats, 0)

    def spread(ref, index, row):
        return jnp.broadcast_to(ref[*index, pl.ds(row, 1), :], (ROWS, LANES))

    def wide(ref, index, row):
        one = spread(ref, index, row)
        return jnp.concatenate([one, one], axis=0).astype(BF)

    def weights(l, row):
        g, r = row // ROWS, row % ROWS
        node = lax.broadcasted_iota(jnp.int32, (NQ, LANES), 0).astype(F32)
        qh = jnp.maximum(0.0, 1.0 - jnp.abs(spread(q_pos_s, (l,), row) - node))
        qh = jnp.concatenate([qh, qh], axis=0).astype(BF)
        parts = []
        for m in range(NT // 2):
            pair = jnp.concatenate(
                [spread(th_s, (g, l, 2 * m), r), spread(th_s, (g, l, 2 * m + 1), r)], axis=0
            ).astype(BF)
            parts.append(pair * qh)
        return jnp.concatenate(parts, axis=0)

    def both(make):
        return jnp.concatenate([make(0), make(1)], axis=1)

    def tile(k):
        return slice(16 * k, 16 * k + 16)

    def put(ref, l, row, total):
        at = pl.ds(pl.multiple_of(row * ROWS, ROWS), ROWS)
        ref[l, at, :] = total[:ROWS] + total[ROWS:]

    def pair_of_rows(p, _):
        def transmit(l, _):
            rhs = both(lambda h: weights(l, 2 * p + h))
            depth = jnp.dot(table_s[l], rhs, preferred_element_type=F32)
            cloud = both(lambda h: wide(c_ref, (l,), 2 * p + h))
            inverse = both(lambda h: wide(inverse_s, (), 2 * p + h))
            for k in range(tiles):
                cond = cond_s[tile(k)]
                part = depth[tile(k)].astype(BF) + jnp.concatenate([cond, cond], axis=1) * cloud
                tr_s[l, tile(k)] = jnp.exp2(part)
                beam_s[l, tile(k)] = jnp.exp2(part * inverse)
            return 0

        unrolled(levels, 30, transmit, 0)

        def pair_tile(ref, k):
            one = ref[tile(k)]
            return jnp.concatenate([one, one], axis=1)

        def put_pair(ref, l, parts):
            total = 0.0
            for k in range(0, tiles, 3):
                total = sum(parts[k + 1 : k + 3], parts[k]).astype(F32) + total
            for h in range(2):
                put(ref, l, 2 * p + h, total[:, h * LANES : (h + 1) * LANES])

        def downward(l, state):
            long, short = (list(part) for part in state)
            step = both(lambda h: wide(dt_s, (l,), 2 * p + h))
            parts = []
            for k in range(tiles):
                kept = tr_s[l, tile(k)] * long[k]
                short[k] = short[k] * beam_s[l, tile(k)]
                long[k] = kept + pair_tile(planck_s, k) * step
                parts.append(kept + short[k])
            put_pair(down_s, l, parts)
            return tuple(long), tuple(short)

        def upward(n, rising):
            l = levels - 1 - n
            step = both(lambda h: wide(dt_s, (jnp.maximum(l - 1, 0),), 2 * p + h))
            rising = list(rising)
            parts = []
            for k in range(tiles):
                risen = tr_s[l, tile(k)] * rising[k]
                rising[k] = risen + pair_tile(planck_s, k) * step
                parts.append(risen)
            put_pair(up_s, l, parts)
            return tuple(rising)

        start = both(lambda h: wide(t_ref, (0,), 2 * p + h))
        start = start * jnp.asarray(-0.25, BF) - jnp.asarray(1.0, BF)
        lit = both(lambda h: wide(lit_s, (), 2 * p + h))
        state = (
            tuple(pair_tile(planck_s, k) * start for k in range(tiles)),
            tuple(pair_tile(insol_s, k) * lit for k in range(tiles)),
        )
        unrolled(levels, 15, downward, state)
        unrolled(levels, 15, upward, (jnp.zeros((16, 2 * LANES), BF),) * tiles)
        return 0

    lax.fori_loop(0, pairs, pair_of_rows, 0)

    def total_of(k):
        return jnp.sum(rounded(points_s[k : k + 1, :]), axis=1, keepdims=True)

    planck_total, insol_total = total_of(0), total_of(1)

    def gathered(ref, l, g):
        base = g * ROWS * ROWS
        return sum(ref[l, pl.ds(base + k, ROWS, stride=ROWS), :] for k in range(ROWS))

    def source_of(l, g):
        return (1.0 + 0.25 * rounded(t_ref[l, g * ROWS : (g + 1) * ROWS])) * planck_total

    def finish(l, carry):
        after = jnp.minimum(l + 1, levels - 1)
        out = []
        for g in range(groups):
            down_in, up_out = carry[g]
            down_out = gathered(down_s, l, g) + source_of(l, g)
            up_in = source_of(after, g) - jnp.where(l == levels - 1, 0.0, gathered(up_s, after, g))
            heat_ref[l, g * ROWS : (g + 1) * ROWS] = (2.0 / gpoints) * (
                down_in - down_out + up_in - up_out
            )
            out.append((down_out, up_in))
        return tuple(out)

    begin = []
    for g in range(groups):
        lit = lit_s[g * ROWS : (g + 1) * ROWS]
        begin.append((lit * insol_total, source_of(0, g) - gathered(up_s, 0, g)))
    ends = unrolled(levels, 3, finish, tuple(begin))
    for g in range(groups):
        surface_s[g * ROWS : (g + 1) * ROWS] = ends[g][0] * (1.0 / gpoints)

    slots_ref[...] = jnp.zeros(slots_ref.shape, F32)

    def clear(h, _):
        taken_s[h] = 0
        return 0

    lax.fori_loop(0, slots_ref.shape[0] // capacity, clear, 0)

    def place(r, _):
        host = hosts_ref[r]
        k = taken_s[host]
        taken_s[host] = k + 1
        slots_ref[pl.ds(host * capacity + k, 1), :] = surface_s[pl.ds(r, 1), :]
        return 0

    lax.fori_loop(0, rows, place, 0)


def pack_edges(t_ref, q_ref, sides_ref, low_ref, high_ref):
    levels, rows, width = t_ref.shape
    lane = lax.broadcasted_iota(jnp.int32, (rows, width), 1) // 2

    def body(l, packed):
        for k, ref in enumerate((t_ref, q_ref)):
            n = k * levels + l
            v = ref[l]
            low_ref[pl.ds(n, 1), :] = v[:1]
            high_ref[pl.ds(n, 1), :] = v[rows - 1 :]
            packed = jnp.where(lane == n, pltpu.roll(v, 2 * n + 1, axis=1), packed)
        return packed

    sides_ref[...] = unrolled(levels, 6, body, jnp.zeros((rows, width), F32))


VMEM_GRANT = 60 * 1024 * 1024


def radiate(hosts, daylight, host_count, capacity, t, q, c, mu, table, planck, insol, cond):
    levels, rows, width = t.shape
    gpoints = table.shape[1]
    padded = -(-gpoints // 16) * 16
    groups = rows // ROWS
    in_vmem = pl.BlockSpec(memory_space=pltpu.VMEM)
    two_rows = pltpu.VMEM((levels, padded, 2 * LANES), BF)
    per_tile = pltpu.VMEM((padded, LANES), BF)
    sums = pltpu.VMEM((levels, rows * ROWS, LANES), F32)
    return pl.pallas_call(
        functools.partial(column_kernel, gpoints, capacity),
        in_specs=[pl.BlockSpec(memory_space=pltpu.SMEM)] * 2 + [in_vmem] * 8,
        out_specs=[in_vmem] * 5,
        out_shape=[
            jax.ShapeDtypeStruct(t.shape, F32),
            jax.ShapeDtypeStruct((host_count * capacity, width), F32),
            jax.ShapeDtypeStruct((rows, width), F32),
            jax.ShapeDtypeStruct((2 * levels, width), F32),
            jax.ShapeDtypeStruct((2 * levels, width), F32),
        ],
        scratch_shapes=[
            pltpu.VMEM((levels, padded, NODES), BF),
            per_tile,
            per_tile,
            per_tile,
            pltpu.VMEM((rows, width), F32),
            pltpu.VMEM((rows, width), F32),
            pltpu.VMEM((ROWS, -(-gpoints // LANES) * LANES), F32),
            pltpu.VMEM((groups, levels, NT, ROWS, LANES), F32),
            pltpu.VMEM((levels, rows, width), F32),
            pltpu.VMEM((levels, rows, width), F32),
            two_rows,
            two_rows,
            sums,
            sums,
            pltpu.VMEM((rows, width), F32),
            pltpu.SMEM((host_count,), jnp.int32),
        ],
        compiler_params=pltpu.CompilerParams(vmem_limit_bytes=VMEM_GRANT),
        cost_estimate=pl.CostEstimate(
            flops=2 * levels * padded * 256 * rows * width,
            bytes_accessed=4 * 4 * levels * rows * width,
            transcendentals=2 * levels * padded * rows * width,
        ),
        name="columns",
    )(hosts, daylight, t, q, c, mu, table, planck[None], insol[None], cond[None])


def chunks(levels):
    count = max(n for n in range(1, 11) if levels % n == 0)
    return count, levels // count


def stencil_kernel(
    levels, t_ref, q_ref, heat_ref, west_ref, east_ref, south_ref, north_ref, t_out, q_out
):
    count, rows, width = t_ref.shape
    lane = lax.broadcasted_iota(jnp.int32, (rows, width), 1)
    row = lax.broadcasted_iota(jnp.int32, (rows, width), 0)

    sides = jnp.where(
        lane % 2 == 0,
        pltpu.roll(east_ref[...], width - 1, axis=1),
        pltpu.roll(west_ref[...], 1, axis=1),
    )

    def smoothed(v, n):
        halo = pltpu.roll(sides, width - 1 - 2 * n, axis=1)
        west = jnp.where(lane == 0, halo, pltpu.roll(v, 1, axis=1))
        east = jnp.where(lane == width - 1, halo, pltpu.roll(v, width - 1, axis=1))
        south = jnp.where(row == 0, south_ref[pl.ds(n, 1), :], pltpu.roll(v, 1, axis=0))
        north = jnp.where(row == rows - 1, north_ref[pl.ds(n, 1), :], pltpu.roll(v, rows - 1, axis=0))
        return v + diffusion * (((north + south) + (east + west)) - 4.0 * v)

    for j in range(count):
        l = pl.program_id(0) * count + j
        t_out[j] = smoothed(t_ref[j], l) + heat_ref[j]
        q_out[j] = smoothed(q_ref[j], levels + l)


def diffuse(t, q, heating, west, east, south, north):
    levels, rows, width = t.shape
    count, steps = chunks(levels)
    block = pl.BlockSpec((count, rows, width), lambda i: (i, 0, 0))

    def whole(x):
        return pl.BlockSpec(x.shape, lambda i: (0, 0))

    out = jax.ShapeDtypeStruct(t.shape, F32)
    return pl.pallas_call(
        functools.partial(stencil_kernel, levels),
        grid=(steps,),
        in_specs=[block, block, block, whole(west), whole(east), whole(south), whole(north)],
        out_specs=[block, block],
        out_shape=[out, out],
        cost_estimate=pl.CostEstimate(
            flops=200 * levels * rows * width * 8,
            bytes_accessed=5 * 4 * levels * rows * width,
            transcendentals=0,
        ),
        name="diffuse",
    )(t, q, heating, west, east, south, north)


def neighbours(low_edge, high_edge, axis):
    count = lax.axis_size(axis)
    forward = [(i, i + 1) for i in range(count - 1)]
    backward = [(target, source) for source, target in forward]
    return lax.ppermute(high_edge, axis, forward), lax.ppermute(low_edge, axis, backward)


def on_device(
    thermal_anomaly_grid,
    relative_moisture,
    overcast_share,
    sun_angle_projection,
    daylight_mask,
    radiator_owner_position,
    molecular_opacity_lookup,
    condensed_opacity_per_share,
    planck_emission_factor,
    insolation_quadrature_factor,
):
    host_count = lax.axis_size("gx")
    t, q = thermal_anomaly_grid, relative_moisture
    blocks = t.shape[1]
    capacity = max(2, (2 * blocks + host_count - 1) // host_count)

    heating, sent, sides, low, high = radiate(
        radiator_owner_position.reshape(blocks),
        daylight_mask.reshape(blocks),
        host_count,
        capacity,
        t,
        q,
        overcast_share,
        sun_angle_projection,
        molecular_opacity_lookup,
        planck_emission_factor,
        insolation_quadrature_factor,
        condensed_opacity_per_share,
    )
    slots = lax.all_to_all(
        sent.reshape(host_count, capacity, sent.shape[1]),
        "gx",
        split_axis=0,
        concat_axis=0,
        tiled=True,
    )
    west, east = neighbours(sides, sides, "gx")
    south, north = neighbours(low, high, "gy")
    t_next, q_next = diffuse(t, q, heating, west, east, south, north)
    return t_next, q_next, slots[None, None]


def solution(mesh):
    placed = (
        P(None, "gy", "gx"),
        P(None, "gy", "gx"),
        P(None, "gy", "gx"),
        P("gy", "gx"),
        P("gx", "gy"),
        P("gx", "gy", None),
        P(),
        P(),
        P(),
        P(),
    )
    return jax.shard_map(
        on_device,
        mesh=mesh,
        in_specs=placed,
        out_specs=(P(None, "gy", "gx"), P(None, "gy", "gx"), P("gy", "gx", None, None, None)),
        check_vma=False,
    )
```
